32 devices in a mesh: grp: 4 (over x, core), seq: 4 (over z), tp: 2 (over y).
Axes of the slice: x: 2, y: 2, z: 4, core: 2. Of those that a mesh axis runs over, the one named last changes fastest.
Arguments:
- hidden: bfloat16 [2048, 8192], P(('grp', 'seq')), may hold values from -6 to 6
- queries: bfloat16 [2048, 4096], P(('grp', 'seq'), 'tp'), may hold values from -900 to 900, as said below
- vis_rows: bfloat16 [16, 4, 4, 8192], P(('grp', 'seq')), may hold values from -6 to 6
- vis_slot: int32 [16, 4, 4], P(('grp', 'seq')), may hold values from -1 to 127, as said below
- doc_ids: int32 [4, 512], P('grp', 'seq'), may hold values from 0 to 7, never falling along the last dimension, each value on 1 to 256 neighbouring positions
- w_key: bfloat16 [8192, 512], P('grp', 'tp'), may hold values from -0.0625 to 0.0625
- w_value: bfloat16 [8192, 512], P('grp', 'tp'), may hold values from -0.0625 to 0.0625
Outputs:
- attended: bfloat16 [2048, 4096], P(('grp', 'seq'), 'tp')
The draws below stay inside these ranges and needn't reach their ends.
Inputs may be any that keep to these rules, and one draw needn't show every extreme that they name: `queries`: a row may be scaled far from one. `vis_slot`: entry [g * 4 + s, d, c] names a position within the 128 positions of index d of seq in group g, or -1. Live positions are distinct within a destination; each device sends 1 to 4 live rows to every destination, slots 0 upward; in every group one destination receives 4 from every device.
All inputs are finite; a program needn't handle non-finite values.
Results may differ from the reference program's by a relative error of at most 0.024.
Values may be sent and summed in bfloat16 or wider, within the bound.
A program may use at most 64 MiB of HBM per device.

```python
import math
import jax
import jax.numpy as jnp
import numpy as np
from jax import lax

D = 8192
HEAD = 128
KVH = 4
QPK = 8
TOK_DEV = 128
CAP = 4
LEN = 512
GROUPS = 4
N_SEQ = 4


def draw_queries(key, part):
    first = jax.random.fold_in(jax.random.fold_in(key, 11), 0)
    base = jnp.clip(jax.random.normal(first, (GROUPS * LEN, KVH * QPK * HEAD), jnp.float32), -6.0, 6.0)
    return base.astype(jnp.bfloat16)


def draw_vis_slot(key, part):
    first, second, third = jax.random.split(jax.random.fold_in(key, 23), 3)
    orders = jax.vmap(lambda one: jax.random.permutation(one, TOK_DEV))(jax.random.split(first, GROUPS * N_SEQ))
    taken = orders[:, :N_SEQ * CAP].reshape(GROUPS, N_SEQ, N_SEQ, CAP).transpose(0, 2, 1, 3)
    counts = jax.random.randint(second, (GROUPS, N_SEQ, N_SEQ), 1, CAP + 1)
    filled = jax.random.randint(third, (GROUPS, 1, 1), 0, N_SEQ)
    target = lax.broadcasted_iota(jnp.int32, (GROUPS, N_SEQ, N_SEQ), 2)
    counts = jnp.where(target == filled, CAP, counts)
    place = lax.broadcasted_iota(jnp.int32, (GROUPS, N_SEQ, N_SEQ, CAP), 3)
    slots = jnp.where(place < counts[..., None], taken, -1)
    return slots.reshape(GROUPS * N_SEQ, N_SEQ, CAP).astype(jnp.int32)


def block_levels(own_key, extent, cuts, least, top_value):
    level = 1.0
    for axis_at, blocks in cuts:
        steps = jax.random.uniform(jax.random.fold_in(jax.random.fold_in(own_key, 6), axis_at), (blocks,), jnp.float32, least / len(cuts), top_value / len(cuts))
        level = level * jnp.repeat(jnp.exp(steps), extent[axis_at] // blocks).reshape((-1,) + (1,) * (len(extent) - 1 - axis_at))
    return level


def length_profile(count, total, limit, lean):
    weights = [(1 << 20) // math.isqrt(rank ** lean) + 1 for rank in range(2, count + 1)]
    surplus, given = total - limit - (count - 1), [1] * (count - 1)
    while surplus > 0:
        free = [i for i in range(count - 1) if given[i] < limit]
        pool, remaining = sum([weights[i] for i in free]), surplus
        for i in free:
            more = min(limit - given[i], max(1, remaining * weights[i] // pool), surplus)
            given[i] = given[i] + more
            surplus = surplus - more
    return np.array([limit] + given)


def ragged_sizes(key, amount, total, reach, lean):
    if amount == 2:
        one = jax.random.randint(key, (), max(1, total - reach), min(reach, total - 1) + 1)
        return jnp.stack([one, total - one])
    tallies = jnp.asarray(length_profile(amount, total, reach, lean), jnp.int32)
    couples = (amount - 1) // 2
    source_of, sink = tallies[1:1 + 2 * couples:2], tallies[2:2 + 2 * couples:2]
    room = jnp.minimum(source_of - 1, reach - sink)
    shifted = jax.random.randint(jax.random.fold_in(key, 1), (couples,), 0, 1 << 20) % (room + 1)
    tallies = tallies.at[1:1 + 2 * couples:2].set(source_of - shifted).at[2:2 + 2 * couples:2].set(sink + shifted)
    return tallies[jax.random.permutation(jax.random.fold_in(key, 2), amount)]


def centred(stream_key, dims, width, reach, cuts=(), kind=jnp.bfloat16):
    drawn = width * jax.random.normal(stream_key, dims, jnp.float32)
    if cuts:
        drawn = drawn * block_levels(stream_key, dims, cuts, -0.22, 0.18)
    return jnp.clip(drawn, -reach, reach).astype(kind)


def setup_inputs(seed: int = 0) -> dict:
    arg_keys = jax.random.split(jax.random.key(seed), 8)
    return {
        "hidden": centred(arg_keys[0], (GROUPS * LEN, D), 1.0, 6.0, ((0, 16),)),
        "queries": draw_queries(jax.random.fold_in(arg_keys[7], 71), 0),
        "vis_rows": centred(arg_keys[2], (GROUPS * N_SEQ, N_SEQ, CAP, D), 1.0, 6.0, ((0, 16),)),
        "vis_slot": draw_vis_slot(jax.random.fold_in(arg_keys[7], 71), 0),
        "doc_ids": jax.vmap(lambda own: jnp.searchsorted(jnp.cumsum(ragged_sizes(own, 8, LEN, LEN // 2, 2)), jnp.arange(LEN), side="right"))(jax.random.split(arg_keys[4], GROUPS)).reshape((GROUPS, LEN)).astype(jnp.int32),
        "w_key": centred(arg_keys[5], (D, KVH * HEAD), D ** -0.5, 0.0625, ((0, 4), (1, 2))),
        "w_value": centred(arg_keys[6], (D, KVH * HEAD), D ** -0.5, 0.0625, ((0, 4), (1, 2))),
    }


def head_attend(q_head, key, value, allowed):
    scores = jnp.dot(q_head, key.T, preferred_element_type=jnp.float32) / jnp.sqrt(jnp.float32(HEAD))
    scores = jnp.where(allowed, scores, jnp.float32(-1e+30))
    top = lax.optimization_barrier(jnp.max(scores, axis=1, keepdims=True))
    weights = jnp.where(allowed, jnp.exp(scores - top), jnp.float32(0.0))
    total = lax.optimization_barrier(jnp.sum(weights, axis=1, keepdims=True))
    mixed = jnp.dot(weights.astype(jnp.bfloat16), value, preferred_element_type=jnp.float32)
    return (mixed / total).astype(jnp.bfloat16)

def one_group(inputs, w_key, w_value):
    hidden, queries, rows, slots, docs = inputs
    text_keys = jnp.dot(hidden, w_key, preferred_element_type=jnp.float32).astype(jnp.bfloat16)
    text_values = jnp.dot(hidden, w_value, preferred_element_type=jnp.float32).astype(jnp.bfloat16)
    flat = rows.reshape(-1, D)
    vis_keys = jnp.dot(flat, w_key, preferred_element_type=jnp.float32).astype(jnp.bfloat16)
    vis_values = jnp.dot(flat, w_value, preferred_element_type=jnp.float32).astype(jnp.bfloat16)
    target = lax.broadcasted_iota(jnp.int32, slots.shape, 1)
    where_to = jnp.where(slots >= 0, target * TOK_DEV + slots, LEN).reshape(-1).astype(jnp.int32)
    keys = text_keys.at[where_to].set(vis_keys, mode='drop')
    values = text_values.at[where_to].set(vis_values, mode='drop')
    places = jnp.arange(LEN, dtype=jnp.int32)
    allowed = (places[None, :] <= places[:, None]) & (docs[None, :] == docs[:, None])
    q_heads = queries.reshape(LEN, KVH, QPK, HEAD).transpose(1, 2, 0, 3)
    k_heads = keys.reshape(LEN, KVH, HEAD).transpose(1, 0, 2)
    v_heads = values.reshape(LEN, KVH, HEAD).transpose(1, 0, 2)

    def per_kv(items):
        q_group, key, value = items
        return lax.map(lambda q_head: head_attend(q_head, key, value, allowed), q_group)
    out = lax.map(per_kv, (q_heads, k_heads, v_heads))
    return out.transpose(2, 0, 1, 3).reshape(LEN, KVH * QPK * HEAD)

def reference(hidden, queries, vis_rows, vis_slot, doc_ids, w_key, w_value):
    stacked = (hidden.reshape(GROUPS, LEN, D), queries.reshape(GROUPS, LEN, KVH * QPK * HEAD), vis_rows.reshape(GROUPS, N_SEQ, N_SEQ, CAP, D), vis_slot.reshape(GROUPS, N_SEQ, N_SEQ, CAP), doc_ids)
    out = lax.map(lambda items: one_group(items, w_key, w_value), stacked)
    return out.reshape(GROUPS * LEN, KVH * QPK * HEAD)
```

```python
import functools

import jax
import jax.numpy as jnp
from jax import lax
from jax.experimental import pallas as pl
from jax.experimental.pallas import tpu as pltpu
from jax.sharding import PartitionSpec as P

HEAD = 128
QPK = 8
F32 = jnp.float32
BF16 = jnp.bfloat16
MESH = pl.DeviceIdType.MESH


def kernel(
    G, S, T,
    hid, vis, qry, wk, wv, pos, docs, out,
    w, hown, hb, part, back, total, kvt, kvv, posb, docb, qs, top, den, acc,
    loc, hs, hr, rs, rr, bs, br, ts, tr, vs, vr, ms, mr,
):
    tok, V = hid.shape[0], vis.shape[0]
    dw, kvc = wk.shape
    nkv = kvc // HEAD
    C = dw // T
    rows = tok + V
    half = tok // 2
    g, s, t = lax.axis_index("grp"), lax.axis_index("seq"), lax.axis_index("tp")
    X = G // 2
    offs = [(ox, oc) for ox in range(X) for oc in range(2) if ox or oc]
    far = [i for i, o in enumerate(offs) if o[0]]
    chunks = [(0, half), (half, rows - half)]

    def to_grp(o, sign):
        ox, oc = o
        return lax.rem(g // 2 + (X + sign * ox), X) * 2 + lax.rem(g % 2 + oc, 2)

    def peer_tp(dt):
        return lax.rem(t + dt, T)

    loads = [
        pltpu.make_async_copy(wk, w.at[:, pl.ds(0, kvc)], loc.at[0]),
        pltpu.make_async_copy(wv, w.at[:, pl.ds(kvc, kvc)], loc.at[1]),
        pltpu.make_async_copy(
            hid.at[:, pl.ds(pl.multiple_of(g * dw, 128), dw)], hown.at[pl.ds(0, tok)], loc.at[2]
        ),
        pltpu.make_async_copy(
            vis.at[:, pl.ds(pl.multiple_of(g * dw, 128), dw)], hown.at[pl.ds(tok, V)], loc.at[3]
        ),
    ]
    qloads = [
        pltpu.make_async_copy(
            qry.at[:, pl.ds((k * QPK + h) * HEAD, HEAD)],
            qs.at[k, pl.ds(h * tok, tok)],
            loc.at[4 + k * QPK + h],
        )
        for k in range(nkv)
        for h in range(QPK)
    ]

    barrier = pltpu.get_barrier_semaphore()
    for o in offs:
        pl.semaphore_signal(barrier, inc=1, device_id={"grp": to_grp(o, 1)}, device_id_type=MESH)
    for d in range(1, S):
        pl.semaphore_signal(
            barrier, inc=1, device_id={"seq": lax.rem(s + d, S)}, device_id_type=MESH
        )
    for d in range(1, T):
        pl.semaphore_signal(barrier, inc=1, device_id={"tp": peer_tp(d)}, device_id_type=MESH)
    for c in loads:
        c.start()
    pl.semaphore_wait(barrier, (G - 1) + (S - 1) + (T - 1))

    def piece(i, ch):
        o = offs[i]
        whom = to_grp(o, 1)
        start = 0 if i not in far else t * C
        wide = dw if i not in far else C
        src_col = pl.multiple_of(whom * dw + start, 128)
        dst_col = pl.multiple_of(start, 128) if i in far else 0
        lo = ch * half
        made = [
            pltpu.make_async_remote_copy(
                src_ref=hid.at[pl.ds(lo, half), pl.ds(src_col, wide)],
                dst_ref=hb.at[i, pl.ds(lo, half), pl.ds(dst_col, wide)],
                send_sem=hs.at[i, ch],
                recv_sem=hr.at[i, ch],
                device_id={"grp": whom},
                device_id_type=MESH,
            )
        ]
        if ch == 1:
            made.append(
                pltpu.make_async_remote_copy(
                    src_ref=vis.at[:, pl.ds(src_col, wide)],
                    dst_ref=hb.at[i, pl.ds(tok, V), pl.ds(dst_col, wide)],
                    send_sem=hs.at[i, 2],
                    recv_sem=hr.at[i, 2],
                    device_id={"grp": whom},
                    device_id_type=MESH,
                )
            )
        return made

    pieces = {(i, ch): piece(i, ch) for i in range(len(offs)) for ch in range(2)}
    items = [(i, ch) for ch in range(2) for i in far]
    near = [i for i in range(len(offs)) if i not in far]
    for it in items + [(i, ch) for i in near for ch in range(2)]:
        for c in pieces[it]:
            c.start()

    posb[pl.ds(pl.multiple_of(s * V, V), V), :] = pos[...]
    docb[s] = docs[...]
    metas = []
    for d in range(1, S):
        whom = lax.rem(s + d, S)
        metas.append(
            pltpu.make_async_remote_copy(
                src_ref=pos, dst_ref=posb.at[pl.ds(pl.multiple_of(s * V, V), V)],
                send_sem=ms.at[d, 0], recv_sem=mr.at[d, 0],
                device_id={"seq": whom}, device_id_type=MESH,
            )
        )
        metas.append(
            pltpu.make_async_remote_copy(
                src_ref=docs, dst_ref=docb.at[s],
                send_sem=ms.at[d, 1], recv_sem=mr.at[d, 1],
                device_id={"seq": whom}, device_id_type=MESH,
            )
        )
    for c in metas:
        c.start()
    for c in qloads:
        c.start()

    for c in loads:
        c.wait()
    total[...] = jnp.dot(hown[...], w[...], preferred_element_type=F32)

    def relay(i, ch):
        lo, n = chunks[ch]
        at = hb.at[i, pl.ds(lo, n), pl.ds(pl.multiple_of(t * C, 128), C)]
        return [
            pltpu.make_async_remote_copy(
                src_ref=at, dst_ref=at,
                send_sem=rs.at[i, ch, d], recv_sem=rr.at[i, ch, d],
                device_id={"tp": peer_tp(d)}, device_id_type=MESH,
            )
            for d in range(1, T)
        ]

    relays = {it: relay(*it) for it in items}

    def giveback(i, ch):
        lo, n = chunks[ch]
        return pltpu.make_async_remote_copy(
            src_ref=part.at[i, pl.ds(lo, n)], dst_ref=back.at[i, pl.ds(lo, n)],
            send_sem=bs.at[i, ch], recv_sem=br.at[i, ch],
            device_id={"grp": to_grp(offs[i], -1)}, device_id_type=MESH,
        )

    gives = {(i, ch): giveback(i, ch) for i in range(len(offs)) for ch in range(2)}

    def project(i, ch):
        lo, n = chunks[ch]
        part[i, lo:lo + n, :] = jnp.dot(
            hb[i, lo:lo + n, :], w[...], preferred_element_type=F32
        ).astype(BF16)
        gives[i, ch].start()

    def finish(it):
        for c in relays[it]:
            c.wait_recv()
        project(*it)

    for at, it in enumerate(items):
        for c in pieces[it]:
            c.wait_recv()
        for c in relays[it]:
            c.start()
        if at == 0:
            for i in near:
                for ch in range(2):
                    for c in pieces[i, ch]:
                        c.wait_recv()
                    project(i, ch)
        else:
            finish(items[at - 1])
    finish(items[-1])

    def text(d, ch):
        here = kvt.at[s, pl.ds(ch * half, half)]
        return pltpu.make_async_remote_copy(
            src_ref=here, dst_ref=here,
            send_sem=ts.at[d, ch], recv_sem=tr.at[s, ch],
            device_id={"seq": d}, device_id_type=MESH,
        )

    vrow = pl.ds(pl.multiple_of(s * V, V), V)

    def visual(d):
        whom = lax.rem(s + d, S)
        return pltpu.make_async_remote_copy(
            src_ref=kvv.at[vrow], dst_ref=kvv.at[vrow],
            send_sem=vs.at[d], recv_sem=vr.at[d],
            device_id={"seq": whom}, device_id_type=MESH,
        )

    visuals = [visual(d) for d in range(1, S)]
    for ch in range(2):
        lo, n = chunks[ch]
        both = total[lo:lo + n, :]
        for i in range(len(offs)):
            gives[i, ch].wait_recv()
            both = both + back[i, lo:lo + n, :].astype(F32)
        both = both.astype(BF16)
        kvt[s, lo:lo + half, :] = both[:half]
        if ch == 1:
            kvv[vrow, :] = both[half:]
            for c in visuals:
                c.start()
        for d in range(S - 1, 0, -1):
            @pl.when(d > s)
            def _():
                text(d, ch).start()

    for c in qloads:
        c.wait()
    for c in metas:
        c.wait_recv()
    for c in visuals:
        c.wait_recv()
    scale = 1.0 / (HEAD ** 0.5)
    lanes = lax.broadcasted_iota(jnp.int32, (S * V, tok), 1)
    krow = lax.broadcasted_iota(jnp.int32, (tok, tok), 0)
    qcol = lax.broadcasted_iota(jnp.int32, (tok, tok), 1)
    qdoc = jnp.broadcast_to(docs[...].astype(F32), (tok, tok))
    top[...] = jnp.full(top.shape, -1e30, F32)
    den[...] = jnp.zeros(den.shape, F32)
    acc[...] = jnp.zeros(acc.shape, F32)
    firsts = (((0,), (0,)), ((), ()))

    def block(j):
        pick = (posb[...] == lanes + j * tok).astype(F32).astype(BF16)
        moved = lax.dot_general(pick, kvv[...], firsts, preferred_element_type=F32)
        used = lax.dot_general(
            pick, jnp.ones((S * V, 2 * kvc), BF16), firsts, preferred_element_type=F32
        )
        kv = jnp.where(used > 0.5, moved, kvt[j].astype(F32)).astype(BF16)
        kdoc = jnp.broadcast_to(docb[j].astype(F32), (tok, tok)).T
        allowed = (krow + j * tok <= qcol + s * tok) & (kdoc == qdoc)
        bias = jnp.where(allowed, F32(0.0), F32(-1e30))
        bias = jnp.concatenate([bias] * QPK, axis=1)
        for k in range(nkv):
            key = kv[:, k * HEAD:(k + 1) * HEAD]
            value = kv[:, kvc + k * HEAD:kvc + (k + 1) * HEAD]
            scores = lax.dot_general(
                key, qs[k], (((1,), (1,)), ((), ())), preferred_element_type=F32
            ) * scale + bias
            old = top[k]
            new = jnp.maximum(old, jnp.max(scores, axis=0, keepdims=True))
            weights = jnp.exp(scores - new)
            shrink = jnp.exp(old - new)
            top[k] = new
            den[k] = den[k] * shrink + jnp.sum(weights, axis=0, keepdims=True)
            acc[k] = acc[k] * shrink + lax.dot_general(
                value, weights.astype(BF16), firsts, preferred_element_type=F32
            )

    block(s)

    def step(i, carry):
        j = s - i
        for ch in range(2):
            there = kvt.at[j, pl.ds(ch * half, half)]
            pltpu.make_async_remote_copy(
                src_ref=there, dst_ref=there,
                send_sem=ts.at[0, ch], recv_sem=tr.at[j, ch],
                device_id={"seq": j}, device_id_type=MESH,
            ).wait_recv()
        block(j)
        return carry

    lax.fori_loop(1, s + 1, step, 0)
    for k in range(nkv):
        done = acc[k] / den[k]
        for h in range(QPK):
            at = (k * QPK + h) * HEAD
            out[:, at:at + HEAD] = done[:, h * tok:(h + 1) * tok].T.astype(out.dtype)

    for it in pieces.values():
        for c in it:
            c.wait_send()
    for it in relays.values():
        for c in it:
            c.wait_send()
    for c in gives.values():
        c.wait_send()
    for c in metas + visuals:
        c.wait_send()
    for ch in range(2):
        for d in range(1, S):
            @pl.when(d > s)
            def _():
                text(d, ch).wait_send()


def shards(G, S, T, hidden, queries, vis_rows, vis_slot, doc_ids, w_key, w_value):
    tok, D = hidden.shape
    vis = vis_rows.reshape(-1, D)
    V = vis.shape[0]
    dw, kvc = w_key.shape
    nkv = kvc // HEAD
    slot = vis_slot.reshape(S, -1)
    place = jnp.arange(S, dtype=jnp.int32)[:, None] * tok + slot
    pos = jnp.where(slot >= 0, place, -1).reshape(V, 1)
    pos = jnp.broadcast_to(pos, (V, tok)).astype(jnp.int32)
    rows = tok + V
    dma = pltpu.SemaphoreType.DMA
    hbm = pl.BlockSpec(memory_space=pl.ANY)
    vmem = pl.BlockSpec(memory_space=pltpu.VMEM)
    return pl.pallas_call(
        functools.partial(kernel, G, S, T),
        out_shape=jax.ShapeDtypeStruct((tok, queries.shape[1]), BF16),
        in_specs=[hbm, hbm, hbm, hbm, hbm, vmem, vmem],
        out_specs=vmem,
        scratch_shapes=[
            pltpu.VMEM((dw, 2 * kvc), BF16),
            pltpu.VMEM((rows, dw), BF16),
            pltpu.VMEM((G - 1, rows, dw), BF16),
            pltpu.VMEM((G - 1, rows, 2 * kvc), BF16),
            pltpu.VMEM((G - 1, rows, 2 * kvc), BF16),
            pltpu.VMEM((rows, 2 * kvc), F32),
            pltpu.VMEM((S, tok, 2 * kvc), BF16),
            pltpu.VMEM((S * V, 2 * kvc), BF16),
            pltpu.VMEM((S * V, tok), jnp.int32),
            pltpu.VMEM((S, 1, tok), jnp.int32),
            pltpu.VMEM((nkv, QPK * tok, HEAD), BF16),
            pltpu.VMEM((nkv, 1, QPK * tok), F32),
            pltpu.VMEM((nkv, 1, QPK * tok), F32),
            pltpu.VMEM((nkv, HEAD, QPK * tok), F32),
            dma((4 + nkv * QPK,)),
            dma((G - 1, 3)), dma((G - 1, 3)),
            dma((G - 1, 2, T)), dma((G - 1, 2, T)),
            dma((G - 1, 2)), dma((G - 1, 2)),
            dma((S, 2)), dma((S, 2)),
            dma((S,)), dma((S,)),
            dma((S, 2)), dma((S, 2)),
        ],
        compiler_params=pltpu.CompilerParams(
            collective_id=0, has_side_effects=True, vmem_limit_bytes=40 * 1024 * 1024
        ),
    )(hidden, vis, queries, w_key, w_value, pos, doc_ids)


def solution(mesh):
    sizes = mesh.shape
    return jax.shard_map(
        functools.partial(shards, sizes["grp"], sizes["seq"], sizes["tp"]),
        mesh=mesh,
        in_specs=(
            P(("grp", "seq"), None),
            P(("grp", "seq"), "tp"),
            P(("grp", "seq"), None, None, None),
            P(("grp", "seq"), None, None),
            P("grp", "seq"),
            P("grp", "tp"),
            P("grp", "tp"),
        ),
        out_specs=P(("grp", "seq"), "tp"),
        check_vma=False,
    )
```

```python
import functools

import jax
import jax.numpy as jnp
from jax import lax
from jax.experimental import pallas as pl
from jax.experimental.pallas import tpu as pltpu
from jax.sharding import PartitionSpec as P

HEAD = 128
QPK = 8
F32 = jnp.float32
BF16 = jnp.bfloat16
MESH = pl.DeviceIdType.MESH


def kernel(
    G, S, T, Q,
    hid, visin, qry, wk, wv, slots, docin, out,
    w, hown, hb, part, back, total, kvt, kvv, posb, docb, qs, top, den, acc,
    visl, vis, slotl, pos, docs,
    loc, hs, hr, rs, rr, bs, br, ts, tr, vs, vr, ms, mr,
):
    tok, V = hid.shape[0], vis.shape[0]
    dw, kvc = wk.shape
    nkv = kvc // HEAD
    cap = V // S
    C = dw // T
    rows = tok + V
    q = tok // Q
    g, s, t = lax.axis_index("grp"), lax.axis_index("seq"), lax.axis_index("tp")
    X = G // 2
    offs = [(ox, oc) for ox in range(X) for oc in range(2) if ox or oc]
    far = [i for i, o in enumerate(offs) if o[0]]
    near = [i for i, o in enumerate(offs) if not o[0]]
    chunks = [(0, V + q)] + [(V + c * q, q) for c in range(1, Q)]
    mine = pl.ds(pl.multiple_of(g * dw, 128), dw)

    def to_grp(o, sign):
        ox, oc = o
        return lax.rem(g // 2 + (X + sign * ox), X) * 2 + lax.rem(g % 2 + oc, 2)

    def peer_tp(dt):
        return lax.rem(t + dt, T)

    first = [
        pltpu.make_async_copy(visin.at[0], visl, loc.at[0]),
        pltpu.make_async_copy(slots.at[0], slotl, loc.at[1]),
        pltpu.make_async_copy(docin, docs, loc.at[2]),
    ]
    loads = [
        pltpu.make_async_copy(hid.at[:, mine], hown.at[pl.ds(V, tok)], loc.at[3]),
        pltpu.make_async_copy(wk, w.at[:, pl.ds(0, kvc)], loc.at[4]),
        pltpu.make_async_copy(wv, w.at[:, pl.ds(kvc, kvc)], loc.at[5]),
    ]
    qloads = [
        pltpu.make_async_copy(
            qry.at[:, pl.ds((k * QPK + h) * HEAD, HEAD)],
            qs.at[k, pl.ds(h * tok, tok)],
            loc.at[6 + k * QPK + h],
        )
        for k in range(nkv)
        for h in range(QPK)
    ]

    barrier = pltpu.get_barrier_semaphore()
    for o in offs:
        pl.semaphore_signal(barrier, inc=1, device_id={"grp": to_grp(o, 1)}, device_id_type=MESH)
    for d in range(1, S):
        pl.semaphore_signal(
            barrier, inc=1, device_id={"seq": lax.rem(s + d, S)}, device_id_type=MESH
        )
    for d in range(1, T):
        pl.semaphore_signal(barrier, inc=1, device_id={"tp": peer_tp(d)}, device_id_type=MESH)
    for c in first + loads:
        c.start()

    for c in first:
        c.wait()
    vis[...] = jnp.concatenate(
        [visl[d].astype(F32) for d in range(S)], axis=0
    ).astype(BF16)
    spread = jnp.concatenate(
        [jnp.broadcast_to(slotl[d:d + 1, :].astype(F32), (cap, cap)) for d in range(S)], axis=0
    )
    r = lax.broadcasted_iota(jnp.int32, (V, cap), 0)
    c = lax.broadcasted_iota(jnp.int32, (V, cap), 1)
    column = jnp.sum(jnp.where(r % cap == c, spread, F32(0.0)), axis=1, keepdims=True)
    column = jnp.broadcast_to(column, (V, tok)).astype(jnp.int32)
    target = lax.broadcasted_iota(jnp.int32, (V, tok), 0) // cap
    pos[...] = jnp.where(column >= 0, column + target * tok, -1)
    pl.semaphore_wait(barrier, (G - 1) + (S - 1) + (T - 1))

    def send(i, src, dst, sem):
        return pltpu.make_async_remote_copy(
            src_ref=src, dst_ref=dst, send_sem=hs.at[i, sem], recv_sem=hr.at[i, sem],
            device_id={"grp": to_grp(offs[i], 1)}, device_id_type=MESH,
        )

    def piece(i, ch):
        whom = to_grp(offs[i], 1)
        start, wide = (t * C, C) if i in far else (0, dw)
        src = pl.ds(pl.multiple_of(whom * dw + start, 128), wide)
        dst = pl.ds(pl.multiple_of(start, 128), wide) if i in far else pl.ds(0, dw)
        lo, n = (ch * q, q) if i in far else (0, tok)
        made = [send(i, hid.at[pl.ds(lo, n), src], hb.at[i, pl.ds(V + lo, n), dst], ch)]
        if ch == 0:
            made.append(send(i, vis.at[:, src], hb.at[i, pl.ds(0, V), dst], Q))
        return made

    pieces = {(i, ch): piece(i, ch) for i in far for ch in range(Q)}
    pieces |= {(i, 0): piece(i, 0) for i in near}

    def launch(ch):
        for i in far:
            for c in pieces[i, ch]:
                c.start()

    launch(0)
    if Q > 1:
        launch(1)
    for i in near:
        for c in pieces[i, 0]:
            c.start()

    vrow = pl.ds(pl.multiple_of(s * V, V), V)
    posb[vrow, :] = pos[...]
    docb[s] = docs[...]
    metas = []
    for d in range(1, S):
        whom = lax.rem(s + d, S)
        for at, (src, dst) in enumerate(((pos, posb.at[vrow]), (docs, docb.at[s]))):
            metas.append(
                pltpu.make_async_remote_copy(
                    src_ref=src, dst_ref=dst, send_sem=ms.at[d, at], recv_sem=mr.at[d, at],
                    device_id={"seq": whom}, device_id_type=MESH,
                )
            )
    for c in metas:
        c.start()
    for c in qloads:
        c.start()

    hown[0:V, :] = vis[:, mine]
    for c in loads:
        c.wait()
    total[...] = jnp.dot(hown[...], w[...], preferred_element_type=F32)

    def relay(i, ch):
        lo, n = chunks[ch]
        at = hb.at[i, pl.ds(lo, n), pl.ds(pl.multiple_of(t * C, 128), C)]
        return [
            pltpu.make_async_remote_copy(
                src_ref=at, dst_ref=at,
                send_sem=rs.at[i, ch, d], recv_sem=rr.at[i, ch, d],
                device_id={"tp": peer_tp(d)}, device_id_type=MESH,
            )
            for d in range(1, T)
        ]

    relays = {(i, ch): relay(i, ch) for i in far for ch in range(Q)}

    def giveback(i, ch):
        lo, n = chunks[ch] if i in far else (0, rows)
        return pltpu.make_async_remote_copy(
            src_ref=part.at[i, pl.ds(lo, n)], dst_ref=back.at[i, pl.ds(lo, n)],
            send_sem=bs.at[i, ch], recv_sem=br.at[i, ch],
            device_id={"grp": to_grp(offs[i], -1)}, device_id_type=MESH,
        )

    gives = {(i, ch): giveback(i, ch) for i in far for ch in range(Q)}
    gives |= {(i, 0): giveback(i, 0) for i in near}

    def finish(ch):
        lo, n = chunks[ch]
        for i in far:
            for c in relays[i, ch]:
                c.wait_recv()
        block = jnp.concatenate([hb[i, lo:lo + n, :] for i in far], axis=0)
        done = jnp.dot(block, w[...], preferred_element_type=F32).astype(BF16)
        for at, i in enumerate(far):
            part[i, lo:lo + n, :] = done[at * n:(at + 1) * n]
            gives[i, ch].start()

    def text(d, ch):
        here = kvt.at[s, pl.ds(ch * q, q)]
        return pltpu.make_async_remote_copy(
            src_ref=here, dst_ref=here,
            send_sem=ts.at[d, ch], recv_sem=tr.at[s, ch],
            device_id={"seq": d}, device_id_type=MESH,
        )

    def visual(d):
        return pltpu.make_async_remote_copy(
            src_ref=kvv.at[vrow], dst_ref=kvv.at[vrow],
            send_sem=vs.at[d], recv_sem=vr.at[d],
            device_id={"seq": lax.rem(s + d, S)}, device_id_type=MESH,
        )

    visuals = [visual(d) for d in range(1, S)]

    def settle(ch):
        lo, n = chunks[ch]
        both = total[lo:lo + n, :]
        for i in range(len(offs)):
            if (i, ch) in gives:
                gives[i, ch].wait_recv()
            both = both + back[i, lo:lo + n, :].astype(F32)
        both = both.astype(BF16)
        kvt[s, ch * q:(ch + 1) * q, :] = both[n - q:]
        if ch == 0:
            kvv[vrow, :] = both[:V]
        for d in range(S - 1, 0, -1):
            @pl.when(d > s)
            def _():
                text(d, ch).start()
        if ch == 0:
            for c in visuals:
                c.start()

    for i in near:
        for c in pieces[i, 0]:
            c.wait_recv()
        part[i] = jnp.dot(hb[i], w[...], preferred_element_type=F32).astype(BF16)
        gives[i, 0].start()
    for ch in range(Q):
        for i in far:
            for c in pieces[i, ch]:
                c.wait_recv()
            for c in relays[i, ch]:
                c.start()
        if ch + 2 < Q:
            launch(ch + 2)
        if ch >= 1:
            finish(ch - 1)
        if ch >= 2:
            settle(ch - 2)
    finish(Q - 1)
    for ch in range(max(Q - 2, 0), Q):
        settle(ch)

    for c in qloads:
        c.wait()
    for c in metas:
        c.wait_recv()
    for c in visuals:
        c.wait_recv()
    scale = 1.0 / (HEAD ** 0.5)
    lanes = lax.broadcasted_iota(jnp.int32, (S * V, tok), 1)
    krow = lax.broadcasted_iota(jnp.int32, (tok, tok), 0)
    qcol = lax.broadcasted_iota(jnp.int32, (tok, tok), 1)
    qdoc = jnp.broadcast_to(docs[...].astype(F32), (tok, tok))
    top[...] = jnp.full(top.shape, -1e30, F32)
    den[...] = jnp.zeros(den.shape, F32)
    acc[...] = jnp.zeros(acc.shape, F32)
    firsts = (((0,), (0,)), ((), ()))

    def block(j):
        pick = (posb[...] == lanes + j * tok).astype(F32).astype(BF16)
        moved = lax.dot_general(pick, kvv[...], firsts, preferred_element_type=F32)
        used = lax.dot_general(
            pick, jnp.ones((S * V, 2 * kvc), BF16), firsts, preferred_element_type=F32
        )
        kv = jnp.where(used > 0.5, moved, kvt[j].astype(F32)).astype(BF16)
        kdoc = jnp.broadcast_to(docb[j].astype(F32), (tok, tok)).T
        allowed = (krow + j * tok <= qcol + s * tok) & (kdoc == qdoc)
        bias = jnp.where(allowed, F32(0.0), F32(-1e30))
        bias = jnp.concatenate([bias] * QPK, axis=1)
        for k in range(nkv):
            key = kv[:, k * HEAD:(k + 1) * HEAD]
            value = kv[:, kvc + k * HEAD:kvc + (k + 1) * HEAD]
            scores = lax.dot_general(
                key, qs[k], (((1,), (1,)), ((), ())), preferred_element_type=F32
            ) * scale + bias
            old = top[k]
            new = jnp.maximum(old, jnp.max(scores, axis=0, keepdims=True))
            weights = jnp.exp(scores - new)
            shrink = jnp.exp(old - new)
            top[k] = new
            den[k] = den[k] * shrink + jnp.sum(weights, axis=0, keepdims=True)
            acc[k] = acc[k] * shrink + lax.dot_general(
                value, weights.astype(BF16), firsts, preferred_element_type=F32
            )

    block(s)

    def step(i, carry):
        j = s - i
        for ch in range(Q):
            there = kvt.at[j, pl.ds(ch * q, q)]
            pltpu.make_async_remote_copy(
                src_ref=there, dst_ref=there,
                send_sem=ts.at[0, ch], recv_sem=tr.at[j, ch],
                device_id={"seq": j}, device_id_type=MESH,
            ).wait_recv()
        block(j)
        return carry

    lax.fori_loop(1, s + 1, step, 0)
    for k in range(nkv):
        done = acc[k] / den[k]
        for h in range(QPK):
            at = (k * QPK + h) * HEAD
            out[:, at:at + HEAD] = done[:, h * tok:(h + 1) * tok].T.astype(out.dtype)

    for it in pieces.values():
        for c in it:
            c.wait_send()
    for it in relays.values():
        for c in it:
            c.wait_send()
    for c in gives.values():
        c.wait_send()
    for c in metas + visuals:
        c.wait_send()
    for ch in range(Q):
        for d in range(1, S):
            @pl.when(d > s)
            def _():
                text(d, ch).wait_send()


def shards(G, S, T, hidden, queries, vis_rows, vis_slot, doc_ids, w_key, w_value):
    tok, D = hidden.shape
    cap = vis_rows.shape[2]
    V = S * cap
    dw, kvc = w_key.shape
    nkv = kvc // HEAD
    Q = 4 if tok % 64 == 0 else 1
    rows = tok + V
    dma = pltpu.SemaphoreType.DMA
    hbm = pl.BlockSpec(memory_space=pltpu.HBM)
    vmem = pl.BlockSpec(memory_space=pltpu.VMEM)
    return pl.pallas_call(
        functools.partial(kernel, G, S, T, Q),
        out_shape=jax.ShapeDtypeStruct((tok, queries.shape[1]), BF16),
        in_specs=[hbm] * 7,
        out_specs=vmem,
        scratch_shapes=[
            pltpu.VMEM((dw, 2 * kvc), BF16),
            pltpu.VMEM((rows, dw), BF16),
            pltpu.VMEM((G - 1, rows, dw), BF16),
            pltpu.VMEM((G - 1, rows, 2 * kvc), BF16),
            pltpu.VMEM((G - 1, rows, 2 * kvc), BF16),
            pltpu.VMEM((rows, 2 * kvc), F32),
            pltpu.VMEM((S, tok, 2 * kvc), BF16),
            pltpu.VMEM((S * V, 2 * kvc), BF16),
            pltpu.VMEM((S * V, tok), jnp.int32),
            pltpu.VMEM((S, 1, tok), jnp.int32),
            pltpu.VMEM((nkv, QPK * tok, HEAD), BF16),
            pltpu.VMEM((nkv, 1, QPK * tok), F32),
            pltpu.VMEM((nkv, 1, QPK * tok), F32),
            pltpu.VMEM((nkv, HEAD, QPK * tok), F32),
            pltpu.VMEM((S, cap, D), BF16),
            pltpu.VMEM((V, D), BF16),
            pltpu.VMEM((S, cap), jnp.int32),
            pltpu.VMEM((V, tok), jnp.int32),
            pltpu.VMEM((1, tok), jnp.int32),
            dma((6 + nkv * QPK,)),
            dma((G - 1, Q + 1)), dma((G - 1, Q + 1)),
            dma((G - 1, Q, T)), dma((G - 1, Q, T)),
            dma((G - 1, Q)), dma((G - 1, Q)),
            dma((S, Q)), dma((S, Q)),
            dma((S,)), dma((S,)),
            dma((S, 2)), dma((S, 2)),
        ],
        compiler_params=pltpu.CompilerParams(
            collective_id=0, has_side_effects=True, vmem_limit_bytes=64 * 1024 * 1024
        ),
    )(hidden, vis_rows, queries, w_key, w_value, vis_slot, doc_ids)


def solution(mesh):
    sizes = mesh.shape
    return jax.shard_map(
        functools.partial(shards, sizes["grp"], sizes["seq"], sizes["tp"]),
        mesh=mesh,
        in_specs=(
            P(("grp", "seq"), None),
            P(("grp", "seq"), "tp"),
            P(("grp", "seq"), None, None, None),
            P(("grp", "seq"), None, None),
            P("grp", "seq"),
            P("grp", "tp"),
            P("grp", "tp"),
        ),
        out_specs=P(("grp", "seq"), "tp"),
        check_vma=False,
    )
```

```python
import functools

import jax
import jax.numpy as jnp
from jax import lax
from jax.experimental import pallas as pl
from jax.experimental.pallas import tpu as pltpu
from jax.sharding import PartitionSpec as P

HEAD = 128
QPK = 8
F32 = jnp.float32
BF16 = jnp.bfloat16
MESH = pl.DeviceIdType.MESH


def kernel(
    G, S, T, Q,
    hid, visin, qry, wk, wv, slots, docin, out,
    w, hown, hb, part, back, total, kvt, kvv, posb, docb, qs, top, den, acc,
    visl, vis, slotl, pos, docs,
    loc, hs, hr, rs, rr, bs, br, ts, tr, vs, vr, ms, mr,
):
    tok, V = hid.shape[0], vis.shape[0]
    dw, kvc = wk.shape
    nkv = kvc // HEAD
    cap = V // S
    C = dw // T
    rows = tok + V
    q = tok // Q
    g, s, t = lax.axis_index("grp"), lax.axis_index("seq"), lax.axis_index("tp")
    X = G // 2
    offs = [(ox, oc) for ox in range(X) for oc in range(2) if ox or oc]
    far = [i for i, o in enumerate(offs) if o[0]]
    near = [i for i, o in enumerate(offs) if not o[0]]
    chunks = [(0, V + q)] + [(V + c * q, q) for c in range(1, Q)]
    mine = pl.ds(pl.multiple_of(g * dw, 128), dw)

    def to_grp(o, sign):
        ox, oc = o
        return lax.rem(g // 2 + (X + sign * ox), X) * 2 + lax.rem(g % 2 + oc, 2)

    def peer_tp(dt):
        return lax.rem(t + dt, T)

    first = [
        pltpu.make_async_copy(visin.at[0], visl, loc.at[0]),
        pltpu.make_async_copy(slots.at[0], slotl, loc.at[1]),
        pltpu.make_async_copy(docin, docs, loc.at[2]),
    ]
    loads = [
        pltpu.make_async_copy(hid.at[:, mine], hown.at[pl.ds(V, tok)], loc.at[3]),
        pltpu.make_async_copy(wk, w.at[:, pl.ds(0, kvc)], loc.at[4]),
        pltpu.make_async_copy(wv, w.at[:, pl.ds(kvc, kvc)], loc.at[5]),
    ]
    qloads = [
        pltpu.make_async_copy(
            qry.at[:, pl.ds((k * QPK + h) * HEAD, HEAD)],
            qs.at[k, pl.ds(h * tok, tok)],
            loc.at[6 + k * QPK + h],
        )
        for k in range(nkv)
        for h in range(QPK)
    ]

    barrier = pltpu.get_barrier_semaphore()
    for o in offs:
        pl.semaphore_signal(barrier, inc=1, device_id={"grp": to_grp(o, 1)}, device_id_type=MESH)
    for d in range(1, S):
        pl.semaphore_signal(
            barrier, inc=1, device_id={"seq": lax.rem(s + d, S)}, device_id_type=MESH
        )
    for d in range(1, T):
        pl.semaphore_signal(barrier, inc=1, device_id={"tp": peer_tp(d)}, device_id_type=MESH)
    for c in first + loads:
        c.start()

    for c in first:
        c.wait()
    vis[...] = jnp.concatenate(
        [visl[d].astype(F32) for d in range(S)], axis=0
    ).astype(BF16)
    spread = jnp.concatenate(
        [jnp.broadcast_to(slotl[d:d + 1, :].astype(F32), (cap, cap)) for d in range(S)], axis=0
    )
    r = lax.broadcasted_iota(jnp.int32, (V, cap), 0)
    c = lax.broadcasted_iota(jnp.int32, (V, cap), 1)
    column = jnp.sum(jnp.where(r % cap == c, spread, F32(0.0)), axis=1, keepdims=True)
    column = jnp.broadcast_to(column, (V, tok)).astype(jnp.int32)
    target = lax.broadcasted_iota(jnp.int32, (V, tok), 0) // cap
    pos[...] = jnp.where(column >= 0, column + target * tok, -1)
    pl.semaphore_wait(barrier, (G - 1) + (S - 1) + (T - 1))

    def send(i, src, dst, sem):
        return pltpu.make_async_remote_copy(
            src_ref=src, dst_ref=dst, send_sem=hs.at[i, sem], recv_sem=hr.at[i, sem],
            device_id={"grp": to_grp(offs[i], 1)}, device_id_type=MESH,
        )

    def piece(i, ch):
        whom = to_grp(offs[i], 1)
        start, wide = (t * C, C) if i in far else (0, dw)
        src = pl.ds(pl.multiple_of(whom * dw + start, 128), wide)
        dst = pl.ds(pl.multiple_of(start, 128), wide) if i in far else pl.ds(0, dw)
        lo, n = (ch * q, q) if i in far else (0, tok)
        made = [send(i, hid.at[pl.ds(lo, n), src], hb.at[i, pl.ds(V + lo, n), dst], ch)]
        if ch == 0:
            made.append(send(i, vis.at[:, src], hb.at[i, pl.ds(0, V), dst], Q))
        return made

    pieces = {(i, ch): piece(i, ch) for i in far for ch in range(Q)}
    pieces |= {(i, 0): piece(i, 0) for i in near}

    def launch(ch):
        for i in far:
            for c in pieces[i, ch]:
                c.start()

    launch(0)
    if Q > 1:
        launch(1)
    vrow = pl.ds(pl.multiple_of(s * V, V), V)
    posb[vrow, :] = pos[...]
    docb[s] = docs[...]
    metas = []
    for d in range(1, S):
        whom = lax.rem(s + d, S)
        for at, (src, dst) in enumerate(((pos, posb.at[vrow]), (docs, docb.at[s]))):
            metas.append(
                pltpu.make_async_remote_copy(
                    src_ref=src, dst_ref=dst, send_sem=ms.at[d, at], recv_sem=mr.at[d, at],
                    device_id={"seq": whom}, device_id_type=MESH,
                )
            )
    for c in metas:
        c.start()
    for c in qloads:
        c.start()

    hown[0:V, :] = vis[:, mine]
    for c in loads:
        c.wait()
    total[...] = jnp.dot(hown[...], w[...], preferred_element_type=F32)

    def relay(i, ch):
        lo, n = chunks[ch]
        at = hb.at[i, pl.ds(lo, n), pl.ds(pl.multiple_of(t * C, 128), C)]
        return [
            pltpu.make_async_remote_copy(
                src_ref=at, dst_ref=at,
                send_sem=rs.at[i, ch, d], recv_sem=rr.at[i, ch, d],
                device_id={"tp": peer_tp(d)}, device_id_type=MESH,
            )
            for d in range(1, T)
        ]

    relays = {(i, ch): relay(i, ch) for i in far for ch in range(Q)}

    def giveback(i, ch):
        lo, n = chunks[ch] if i in far else (0, rows)
        return pltpu.make_async_remote_copy(
            src_ref=part.at[i, pl.ds(lo, n)], dst_ref=back.at[i, pl.ds(lo, n)],
            send_sem=bs.at[i, ch], recv_sem=br.at[i, ch],
            device_id={"grp": to_grp(offs[i], -1)}, device_id_type=MESH,
        )

    gives = {(i, ch): giveback(i, ch) for i in far for ch in range(Q)}
    gives |= {(i, 0): giveback(i, 0) for i in near}

    def finish(ch):
        lo, n = chunks[ch]
        for i in far:
            for c in relays[i, ch]:
                c.wait_recv()
        block = jnp.concatenate([hb[i, lo:lo + n, :] for i in far], axis=0)
        done = jnp.dot(block, w[...], preferred_element_type=F32).astype(BF16)
        for at, i in enumerate(far):
            part[i, lo:lo + n, :] = done[at * n:(at + 1) * n]
            gives[i, ch].start()

    def text(d, ch):
        here = kvt.at[s, pl.ds(ch * q, q)]
        return pltpu.make_async_remote_copy(
            src_ref=here, dst_ref=here,
            send_sem=ts.at[d, ch], recv_sem=tr.at[s, ch],
            device_id={"seq": d}, device_id_type=MESH,
        )

    def visual(d):
        return pltpu.make_async_remote_copy(
            src_ref=kvv.at[vrow], dst_ref=kvv.at[vrow],
            send_sem=vs.at[d], recv_sem=vr.at[d],
            device_id={"seq": lax.rem(s + d, S)}, device_id_type=MESH,
        )

    visuals = [visual(d) for d in range(1, S)]

    def settle(ch):
        lo, n = chunks[ch]
        both = total[lo:lo + n, :]
        for i in range(len(offs)):
            if (i, ch) in gives:
                gives[i, ch].wait_recv()
            both = both + back[i, lo:lo + n, :].astype(F32)
        both = both.astype(BF16)
        kvt[s, ch * q:(ch + 1) * q, :] = both[n - q:]
        if ch == 0:
            kvv[vrow, :] = both[:V]
        for d in range(1, S):
            @pl.when(d > s)
            def _():
                text(d, ch).start()
        if ch == 0:
            for c in visuals:
                c.start()

    for i in near:
        for c in pieces[i, 0]:
            c.start()
    for i in near:
        for c in pieces[i, 0]:
            c.wait_recv()
        part[i] = jnp.dot(hb[i], w[...], preferred_element_type=F32).astype(BF16)
        gives[i, 0].start()
    for ch in range(Q):
        for i in far:
            for c in pieces[i, ch]:
                c.wait_recv()
            for c in relays[i, ch]:
                c.start()
        if ch >= 1:
            finish(ch - 1)
        if ch + 2 < Q:
            launch(ch + 2)
        if ch >= 2:
            settle(ch - 2)
    finish(Q - 1)
    for ch in range(max(Q - 2, 0), Q):
        settle(ch)

    for c in qloads:
        c.wait()
    for c in metas:
        c.wait_recv()
    for c in visuals:
        c.wait_recv()
    scale = 1.0 / (HEAD ** 0.5)
    lanes = lax.broadcasted_iota(jnp.int32, (S * V, tok), 1)
    krow = lax.broadcasted_iota(jnp.int32, (tok, tok), 0)
    qcol = lax.broadcasted_iota(jnp.int32, (tok, tok), 1)
    qdoc = jnp.broadcast_to(docs[...].astype(F32), (tok, tok))
    top[...] = jnp.full(top.shape, -1e30, F32)
    den[...] = jnp.zeros(den.shape, F32)
    acc[...] = jnp.zeros(acc.shape, F32)
    firsts = (((0,), (0,)), ((), ()))

    def block(j):
        pick = (posb[...] == lanes + j * tok).astype(F32).astype(BF16)
        moved = lax.dot_general(pick, kvv[...], firsts, preferred_element_type=F32)
        used = lax.dot_general(
            pick, jnp.ones((S * V, 2 * kvc), BF16), firsts, preferred_element_type=F32
        )
        kv = jnp.where(used > 0.5, moved, kvt[j].astype(F32)).astype(BF16)
        kdoc = jnp.broadcast_to(docb[j].astype(F32), (tok, tok)).T
        allowed = (krow + j * tok <= qcol + s * tok) & (kdoc == qdoc)
        bias = jnp.where(allowed, F32(0.0), F32(-1e30))
        bias = jnp.concatenate([bias] * QPK, axis=1)
        for k in range(nkv):
            key = kv[:, k * HEAD:(k + 1) * HEAD]
            value = kv[:, kvc + k * HEAD:kvc + (k + 1) * HEAD]
            scores = lax.dot_general(
                key, qs[k], (((1,), (1,)), ((), ())), preferred_element_type=F32
            ) * scale + bias
            old = top[k]
            new = jnp.maximum(old, jnp.max(scores, axis=0, keepdims=True))
            weights = jnp.exp(scores - new)
            shrink = jnp.exp(old - new)
            top[k] = new
            den[k] = den[k] * shrink + jnp.sum(weights, axis=0, keepdims=True)
            acc[k] = acc[k] * shrink + lax.dot_general(
                value, weights.astype(BF16), firsts, preferred_element_type=F32
            )

    block(s)

    def step(i, carry):
        j = s - i
        for ch in range(Q):
            there = kvt.at[j, pl.ds(ch * q, q)]
            pltpu.make_async_remote_copy(
                src_ref=there, dst_ref=there,
                send_sem=ts.at[0, ch], recv_sem=tr.at[j, ch],
                device_id={"seq": j}, device_id_type=MESH,
            ).wait_recv()
        block(j)
        return carry

    lax.fori_loop(1, s + 1, step, 0)
    for k in range(nkv):
        done = acc[k] / den[k]
        for h in range(QPK):
            at = (k * QPK + h) * HEAD
            out[:, at:at + HEAD] = done[:, h * tok:(h + 1) * tok].T.astype(out.dtype)

    for it in pieces.values():
        for c in it:
            c.wait_send()
    for it in relays.values():
        for c in it:
            c.wait_send()
    for c in gives.values():
        c.wait_send()
    for c in metas + visuals:
        c.wait_send()
    for ch in range(Q):
        for d in range(1, S):
            @pl.when(d > s)
            def _():
                text(d, ch).wait_send()


def shards(G, S, T, hidden, queries, vis_rows, vis_slot, doc_ids, w_key, w_value):
    tok, D = hidden.shape
    cap = vis_rows.shape[2]
    V = S * cap
    dw, kvc = w_key.shape
    nkv = kvc // HEAD
    Q = 4 if tok % 64 == 0 else 1
    rows = tok + V
    dma = pltpu.SemaphoreType.DMA
    hbm = pl.BlockSpec(memory_space=pltpu.HBM)
    vmem = pl.BlockSpec(memory_space=pltpu.VMEM)
    return pl.pallas_call(
        functools.partial(kernel, G, S, T, Q),
        out_shape=jax.ShapeDtypeStruct((tok, queries.shape[1]), BF16),
        in_specs=[hbm] * 7,
        out_specs=vmem,
        scratch_shapes=[
            pltpu.VMEM((dw, 2 * kvc), BF16),
            pltpu.VMEM((rows, dw), BF16),
            pltpu.VMEM((G - 1, rows, dw), BF16),
            pltpu.VMEM((G - 1, rows, 2 * kvc), BF16),
            pltpu.VMEM((G - 1, rows, 2 * kvc), BF16),
            pltpu.VMEM((rows, 2 * kvc), F32),
            pltpu.VMEM((S, tok, 2 * kvc), BF16),
            pltpu.VMEM((S * V, 2 * kvc), BF16),
            pltpu.VMEM((S * V, tok), jnp.int32),
            pltpu.VMEM((S, 1, tok), jnp.int32),
            pltpu.VMEM((nkv, QPK * tok, HEAD), BF16),
            pltpu.VMEM((nkv, 1, QPK * tok), F32),
            pltpu.VMEM((nkv, 1, QPK * tok), F32),
            pltpu.VMEM((nkv, HEAD, QPK * tok), F32),
            pltpu.VMEM((S, cap, D), BF16),
            pltpu.VMEM((V, D), BF16),
            pltpu.VMEM((S, cap), jnp.int32),
            pltpu.VMEM((V, tok), jnp.int32),
            pltpu.VMEM((1, tok), jnp.int32),
            dma((6 + nkv * QPK,)),
            dma((G - 1, Q + 1)), dma((G - 1, Q + 1)),
            dma((G - 1, Q, T)), dma((G - 1, Q, T)),
            dma((G - 1, Q)), dma((G - 1, Q)),
            dma((S, Q)), dma((S, Q)),
            dma((S,)), dma((S,)),
            dma((S, 2)), dma((S, 2)),
        ],
        compiler_params=pltpu.CompilerParams(
            collective_id=0, has_side_effects=True, vmem_limit_bytes=64 * 1024 * 1024
        ),
    )(hidden, vis_rows, queries, w_key, w_value, vis_slot, doc_ids)


def solution(mesh):
    sizes = mesh.shape
    return jax.shard_map(
        functools.partial(shards, sizes["grp"], sizes["seq"], sizes["tp"]),
        mesh=mesh,
        in_specs=(
            P(("grp", "seq"), None),
            P(("grp", "seq"), "tp"),
            P(("grp", "seq"), None, None, None),
            P(("grp", "seq"), None, None),
            P("grp", "seq"),
            P("grp", "tp"),
            P("grp", "tp"),
        ),
        out_specs=P(("grp", "seq"), "tp"),
        check_vma=False,
    )
```
